768 devices in a mesh: member: 8 (over y_lo, core), shard: 96 (over z, x, y_hi).
Axes of the slice: x: 4, y: 8 (y_hi: 2, y_lo: 4; y = y_hi * 4 + y_lo), z: 12, core: 2. Of those that a mesh axis runs over, the one named last changes fastest.
Arguments:
- latents: bfloat16 [16, 12288, 1024], P('member', 'shard'), may hold values from -8 to 8
- queries: bfloat16 [16, 12288, 1024], P('member', 'shard'), may hold values from -48 to 48
- neighbours: int32 [12288, 4], P('shard'), may hold values from 0 to 12287, as said below
- truth: float32 [12288, 100], P('shard'), may hold values from -6 to 6
- area_weight: float32 [12288], P('shard'), may hold values from 0.25 to 2.5
- var_weight: float32 [100], replicated, may hold values from 0.25 to 2.5
- proj_weight: bfloat16 [1024, 100], replicated, may hold values from -0.1875 to 0.1875
Outputs:
- latent_grad: bfloat16 [16, 12288, 1024], P('member', 'shard')
- proj_grad: float32 [1024, 100], replicated
The draws below stay inside these ranges and needn't reach their ends.
Inputs may be any that keep to these rules, and one draw needn't show every extreme that they name: The neighbours of a point of block s (points s * 128 to (s + 1) * 128 - 1) lie among nodes s * 128 - 32 to (s + 1) * 128 + 31, taken modulo 12288; the first point of each block names both ends of that range.
All inputs are finite; a program needn't handle non-finite values.
Results may differ from the reference program's by a relative error of at most 0.0079.
Values may be sent and summed in bfloat16 or wider, within the bound.
No kernel may reach another device: no remote copies, remote signals or barrier semaphores. Data moves between devices by JAX's collectives and lax.ppermute only.
A program may use at most 32 MiB of HBM per device.

```python
import math
import jax
import jax.numpy as jnp
from jax import lax

D = 1024
VARS = 100
PTS_DEV = 128
NODES_DEV = 128
DEG = 4
MEMBERS = 16
HALO = 32
POINTS = 12288
NODES = 12288


def neighbour_table(key):
    key = jax.random.fold_in(key, 101)
    offsets = jax.random.randint(key, (POINTS, DEG), -HALO, NODES_DEV + HALO)
    column = jnp.arange(DEG)[None, :]
    forced = jnp.where(column == 0, -HALO, jnp.where(column == 1, NODES_DEV + HALO - 1, offsets))
    first = (jnp.arange(POINTS) % PTS_DEV == 0)[:, None]
    offsets = jnp.where(first, forced, offsets)
    block = (jnp.arange(POINTS) // PTS_DEV)[:, None]
    return ((block * NODES_DEV + offsets) % NODES).astype(jnp.int32)


def latent_base(key):
    key = jax.random.fold_in(key, 202)
    return jnp.clip(jax.random.normal(key, (MEMBERS, NODES, D), jnp.float32), -6.0, 6.0)


def draw_neighbours(key, part):
    return neighbour_table(key)


def draw_latents(key, part):
    base = latent_base(key)
    return base.astype(jnp.bfloat16)


def draw_queries(key, part):
    key = jax.random.fold_in(key, 8)
    values = jnp.clip(jax.random.normal(key, (MEMBERS, POINTS, D), jnp.float32), -6.0, 6.0)
    return values.astype(jnp.bfloat16)


def level_of(key, shape, shards, low, largest):
    factor_of, own = 1.0, jax.random.fold_in(key, 6)
    for dim, blocks in shards:
        steps = jnp.exp(jax.random.uniform(jax.random.fold_in(own, dim), (blocks,), jnp.float32, low / len(shards), largest / len(shards)))
        factor_of = factor_of * jnp.repeat(steps, shape[dim] // blocks).reshape([-1 if axis == dim else 1 for axis in range(len(shape))])
    return factor_of


def normal_values(stream_key, extent, scale, limit, cuts=(), kind=jnp.bfloat16):
    result = scale * jax.random.normal(stream_key, extent, jnp.float32)
    if cuts:
        result = result * level_of(stream_key, extent, cuts, -0.22, 0.18)
    return jnp.clip(result, -limit, limit).astype(kind)


def setup_inputs(seed: int = 0) -> dict:
    key_list = jax.random.split(jax.random.key(seed), 8)
    return {
        "latents": draw_latents(jax.random.fold_in(key_list[7], 71), 0),
        "queries": draw_queries(jax.random.fold_in(key_list[7], 71), 0),
        "neighbours": draw_neighbours(jax.random.fold_in(key_list[7], 71), 0),
        "truth": normal_values(key_list[3], (POINTS, VARS), 1.0, 6.0, ((0, 96),), jnp.float32),
        "area_weight": jnp.clip(jnp.exp(math.log(2.5) - 2.3025851 * jax.random.uniform(key_list[4], (POINTS,), jnp.float32) ** level_of(key_list[4], (POINTS,), ((0, 96),), -0.2, 0.2)), 0.25, 2.5),
        "var_weight": jnp.clip(jnp.exp(jax.random.uniform(key_list[5], (VARS,), jnp.float32, math.log(0.25), math.log(2.5))), 0.25, 2.5),
        "proj_weight": normal_values(key_list[6], (D, VARS), D ** -0.5, 0.1875),
    }


smoothing = 0.25
fairness = 0.95

def slope(diff):
    return diff * lax.rsqrt(diff * diff + smoothing * smoothing)

def crps_grad(ensemble, own_part, target, weighting):
    count = ensemble.shape[0]
    eps_fair = (1.0 - fairness) / count
    spread = jnp.zeros(own_part.shape, jnp.float32)
    for other in range(count):
        spread = spread + slope(own_part - ensemble[other][None])
    skill = slope(own_part - target[None])
    return weighting[None] * (skill / count - (1.0 - eps_fair) / (count * (count - 1)) * spread)

def reference(latents, queries, neighbours, truth, area_weight, var_weight, proj_weight):
    score_scale = 1.0 / math.sqrt(D)

    def forward(member_lat, member_query):
        rows = [member_lat[neighbours[:, slot]] for slot in range(DEG)]
        scores = jnp.stack([lax.optimization_barrier(jnp.sum(member_query.astype(jnp.float32) * rows_j.astype(jnp.float32), -1)) for rows_j in rows]) * score_scale
        attn = jax.nn.softmax(scores, axis=0)
        mixed = member_query.astype(jnp.float32)
        for slot in range(DEG):
            mixed = mixed + attn[slot][:, None] * rows[slot].astype(jnp.float32)
        return (rows, attn, mixed.astype(jnp.bfloat16))

    def predict(pair):
        mixed = forward(pair[0], pair[1])[2]
        return jnp.dot(mixed, proj_weight, preferred_element_type=jnp.float32)
    pred = lax.map(predict, (latents, queries))
    weighting = area_weight[:, None] * var_weight[None, :]
    dpred = crps_grad(pred, pred, truth, weighting)

    def backward(triple):
        member_lat, member_query, member_grad = triple
        rows, attn, mixed = forward(member_lat, member_query)
        grad_b = member_grad.astype(jnp.bfloat16)
        weight_term = lax.dot_general(mixed, grad_b, (((0,), (0,)), ((), ())), preferred_element_type=jnp.float32)
        dmixed = lax.dot_general(grad_b, proj_weight, (((1,), (1,)), ((), ())), preferred_element_type=jnp.float32).astype(jnp.bfloat16)
        dattn = jnp.stack([lax.optimization_barrier(jnp.sum(dmixed.astype(jnp.float32) * rows_j.astype(jnp.float32), -1)) for rows_j in rows])
        dscores = attn * (dattn - lax.optimization_barrier(jnp.sum(attn * dattn, axis=0))[None])
        node_grad = jnp.zeros((NODES, D), jnp.float32)
        for slot in range(DEG):
            contrib = attn[slot][:, None] * dmixed.astype(jnp.float32) + (dscores[slot] * score_scale)[:, None] * member_query.astype(jnp.float32)
            node_grad = node_grad.at[neighbours[:, slot]].add(contrib)
        return (node_grad.astype(jnp.bfloat16), weight_term)
    latent_grad, weight_terms = lax.map(backward, (latents, queries, dpred))
    return (latent_grad, lax.optimization_barrier(jnp.sum(weight_terms, axis=0)))
```

```python
import functools
import math

import jax
import jax.numpy as jnp
from jax import lax
from jax.experimental import pallas as pl
from jax.experimental.pallas import tpu as pltpu
from jax.sharding import Mesh, PartitionSpec as P

smoothing = 0.25
fairness = 0.95
LANES = 128
f32, bf16 = jnp.float32, jnp.bfloat16

MEMBER = ("ylo", "core")
SHARD = ("z", "x", "yhi")
SPREAD = ("x", "ylo", "core")
VMEM_LIMIT = 48 * 1024 * 1024


def slope(diff):
    return diff * lax.rsqrt(diff * diff + smoothing * smoothing)


def dot(a, b, ca, cb):
    return lax.dot_general(a, b, (((ca,), (cb,)), ((), ())), preferred_element_type=f32)


def halves(x):
    high = x.astype(bf16)
    return high, (x - high.astype(f32)).astype(bf16)


def fill_window(window, m, own, low, high):
    nodes, reach = own.shape[1], low.shape[1]
    window[0:nodes] = own[m]
    window[nodes : nodes + reach] = low[m]
    window[nodes + reach : nodes + 2 * reach] = high[m]


def forward_kernel(
    scale, slots, own, low, high, queries, weight, attn_out, mixed_out, pred_out, window
):
    members, points, _ = queries.shape
    rows = window.shape[0]
    nodes, reach = own.shape[1], low.shape[1]
    share = pred_out.shape[2]
    window[nodes + 2 * reach :] = jnp.zeros((rows - nodes - 2 * reach, window.shape[1]), bf16)
    place = lax.broadcasted_iota(jnp.int32, (rows, points), 0)
    count = jnp.zeros((rows, points), f32)
    for slot in range(slots.shape[0]):
        count = count + (place == slots[slot : slot + 1]).astype(f32)
    used = count > 0.0
    for m in range(members):
        fill_window(window, m, own, low, high)
        scores = dot(window[...], queries[m], 1, 1) * scale
        scores = jnp.where(used, scores, -1e30)
        top = jnp.max(scores, axis=0, keepdims=True)
        raised = count * jnp.exp(scores - top)
        attn = raised / jnp.sum(raised, axis=0, keepdims=True)
        attn_out[m] = attn
        attn_high, attn_low = halves(attn)
        mixed = queries[m].astype(f32) + (
            dot(attn_high, window[...], 0, 0) + dot(attn_low, window[...], 0, 0)
        )
        mixed = mixed.astype(bf16)
        mixed_out[m] = mixed
        pred = dot(mixed, weight[...], 1, 1)
        for k in range(points // share):
            pred_out[k, m] = pred[k * share : (k + 1) * share]


def crps_kernel(rows, target, weighting, out):
    groups, each, share, lanes = rows.shape
    count = groups * each
    eps_fair = (1.0 - fairness) / count
    values = [rows[k // each, k % each] for k in range(count)]
    spread = [jnp.zeros((share, lanes), f32) for _ in range(count)]
    for a in range(count):
        for b in range(a + 1, count):
            s = slope(values[a] - values[b])
            spread[a] = spread[a] + s
            spread[b] = spread[b] - s
    for k in range(count):
        skill = slope(values[k] - target[...])
        grad = weighting[...] * (
            skill / count - (1.0 - eps_fair) / (count * (count - 1)) * spread[k]
        )
        out[k // each, k % each] = grad.astype(bf16)


def weight_kernel(grads, mixed, out):
    owners, members, share, lanes = grads.shape
    points = owners * share
    total = None
    for m in range(members):
        g = grads[:, m].reshape(points, lanes)
        term = dot(g, mixed[m], 0, 0)
        total = term if total is None else total + term
    pieces, high, wide = out.shape
    across = total.shape[1] // wide
    for k in range(pieces):
        r, c = k // across * high, k % across * wide
        out[k] = total[r : r + high, c : c + wide].astype(bf16)


def backward_kernel(
    scale, grads, attn, own, low, high, queries, weight, own_out, low_out, high_out, window
):
    owners, members, share, lanes = grads.shape
    points = owners * share
    rows = window.shape[0]
    nodes, reach = own.shape[1], low.shape[1]
    window[nodes + 2 * reach :] = jnp.zeros((rows - nodes - 2 * reach, window.shape[1]), bf16)
    for m in range(members):
        fill_window(window, m, own, low, high)
        g = grads[:, m].reshape(points, lanes)
        dmixed = dot(g, weight[...], 1, 0).astype(bf16)
        dattn = dot(window[...], dmixed, 1, 1)
        a = attn[m]
        dscores = a * (dattn - jnp.sum(a * dattn, axis=0, keepdims=True)) * scale
        a_high, a_low = halves(a)
        s_high, s_low = halves(dscores)
        total = (
            dot(a_high, dmixed, 1, 0)
            + dot(s_high, queries[m], 1, 0)
            + dot(a_low, dmixed, 1, 0)
            + dot(s_low, queries[m], 1, 0)
        )
        own_out[m] = total[:nodes]
        low_out[m] = total[nodes : nodes + reach].astype(bf16)
        high_out[m] = total[nodes + reach : nodes + 2 * reach].astype(bf16)


def finish_kernel(own, from_prev, from_next, out):
    nodes, reach = own.shape[1], from_prev.shape[1]
    for m in range(own.shape[0]):
        out[m, :reach] = (own[m, :reach] + from_prev[m].astype(f32)).astype(bf16)
        out[m, reach : nodes - reach] = own[m, reach : nodes - reach].astype(bf16)
        out[m, nodes - reach :] = (own[m, nodes - reach :] + from_next[m].astype(f32)).astype(bf16)


def call(kernel, out_shape, args, scratch=(), name=None):
    vmem = pl.BlockSpec(memory_space=pltpu.VMEM)
    single = not isinstance(out_shape, (list, tuple))
    return pl.pallas_call(
        kernel,
        out_shape=out_shape,
        in_specs=[vmem] * len(args),
        out_specs=vmem if single else [vmem] * len(out_shape),
        scratch_shapes=list(scratch),
        compiler_params=pltpu.CompilerParams(vmem_limit_bytes=VMEM_LIMIT),
        name=name,
    )(*args)


def spread_out(x, axes):
    count = lax.axis_size(axes)
    return lax.all_to_all(jnp.broadcast_to(x[None], (count,) + x.shape), axes, 0, 0, tiled=True)


def local(latents, queries, neighbours, truth, area_weight, var_weight, proj_weight):
    members, nodes, width = latents.shape
    points = queries.shape[1]
    variables = proj_weight.shape[1]
    reach = nodes // 4
    scale = 1.0 / math.sqrt(width)
    shards = lax.axis_size(SHARD)
    owners = lax.axis_size(MEMBER)
    share = points // owners
    forward = [(i, (i + 1) % shards) for i in range(shards)]
    backward = [(i, (i - 1) % shards) for i in range(shards)]

    low = lax.ppermute(latents[:, nodes - reach :], SHARD, forward)
    high = lax.ppermute(latents[:, :reach], SHARD, backward)

    first = lax.axis_index(SHARD) * nodes
    index = (neighbours.T - first + reach) % (nodes * shards)
    slots = jnp.where(
        index < reach, index + nodes, jnp.where(index < nodes + reach, index - reach, index)
    )
    weight = jnp.pad(proj_weight.T, ((0, LANES - variables), (0, 0)))
    start = lax.axis_index(MEMBER) * share
    pad_lanes = ((0, 0), (0, LANES - variables))
    target = jnp.pad(lax.dynamic_slice_in_dim(truth, start, share, 0), pad_lanes)
    area = lax.dynamic_slice_in_dim(area_weight, start, share, 0)
    weighting = jnp.pad(area[:, None] * var_weight[None, :], pad_lanes)

    window_rows = 2 * LANES
    window = pltpu.VMEM((window_rows, width), bf16)
    attn, mixed, pred = call(
        functools.partial(forward_kernel, scale),
        [
            jax.ShapeDtypeStruct((members, window_rows, points), f32),
            jax.ShapeDtypeStruct((members, points, width), bf16),
            jax.ShapeDtypeStruct((owners, members, share, LANES), f32),
        ],
        (slots, latents, low, high, queries, weight),
        [window],
        name="forward",
    )
    rows = lax.all_to_all(pred, MEMBER, 0, 0, tiled=True)
    owner_grad = call(
        crps_kernel,
        jax.ShapeDtypeStruct(rows.shape, bf16),
        (rows, target, weighting),
        name="crps",
    )
    grads = lax.all_to_all(owner_grad, MEMBER, 0, 0, tiled=True)

    across = width // LANES
    pieces = lax.axis_size(SPREAD)
    tall = LANES // (pieces // across)
    term = call(
        weight_kernel,
        jax.ShapeDtypeStruct((pieces, tall, LANES), bf16),
        (grads, mixed),
        name="weight_term",
    )
    term = lax.all_to_all(term, SPREAD, 0, 0, tiled=True)

    own_part, low_part, high_part = call(
        functools.partial(backward_kernel, scale),
        [
            jax.ShapeDtypeStruct((members, nodes, width), f32),
            jax.ShapeDtypeStruct((members, reach, width), bf16),
            jax.ShapeDtypeStruct((members, reach, width), bf16),
        ],
        (grads, attn, latents, low, high, queries, weight),
        [window],
        name="backward",
    )
    term, low_part, high_part = lax.optimization_barrier((term, low_part, high_part))
    from_next = lax.ppermute(low_part, SHARD, backward)
    from_prev = lax.ppermute(high_part, SHARD, forward)

    piece = jnp.sum(term.astype(f32), axis=0).astype(bf16)
    piece = jnp.sum(spread_out(piece, "z").astype(f32), axis=0)
    piece = piece + lax.ppermute(piece, "yhi", [(0, 1), (1, 0)])
    piece, from_next, from_prev = lax.optimization_barrier((piece, from_next, from_prev))
    full = spread_out(piece.astype(bf16), SPREAD).astype(f32)
    full = full.reshape(pieces // across, across, tall, LANES).transpose(0, 2, 1, 3)
    proj_grad = full.reshape(LANES, width)[:variables].T

    latent_grad = call(
        finish_kernel,
        jax.ShapeDtypeStruct(latents.shape, bf16),
        (own_part, from_prev, from_next),
        name="finish",
    )
    return latent_grad, proj_grad


def solution(mesh):
    fine = Mesh(mesh.devices.reshape(4, 2, 12, 4, 2), MEMBER + SHARD)
    placed = (
        P(MEMBER, SHARD, None),
        P(MEMBER, SHARD, None),
        P(SHARD, None),
        P(SHARD, None),
        P(SHARD),
        P(),
        P(),
    )
    return jax.shard_map(
        local,
        mesh=fine,
        in_specs=placed,
        out_specs=(P(MEMBER, SHARD, None), P()),
        check_vma=False,
    )
```

```python
import functools
import math

import jax
import jax.numpy as jnp
from jax import lax
from jax.experimental import pallas as pl
from jax.experimental.pallas import tpu as pltpu
from jax.sharding import Mesh, PartitionSpec as P

smoothing = 0.25
fairness = 0.95
LANES = 128
f32, bf16 = jnp.float32, jnp.bfloat16

MEMBER = ("ylo", "core")
SHARD = ("z", "x", "yhi")
SPREAD = ("x", "ylo", "yhi")
VMEM_LIMIT = 48 * 1024 * 1024


def slope(diff):
    return diff * lax.rsqrt(diff * diff + smoothing * smoothing)


def dot(a, b, ca, cb):
    return lax.dot_general(a, b, (((ca,), (cb,)), ((), ())), preferred_element_type=f32)


def halves(x):
    high = x.astype(bf16)
    return high, (x - high.astype(f32)).astype(bf16)


def fill_window(window, m, own, low, high):
    nodes, reach = own.shape[1], low.shape[1]
    window[0:nodes] = own[m]
    window[nodes : nodes + reach] = low[m]
    window[nodes + reach : nodes + 2 * reach] = high[m]


def forward_kernel(
    scale, core, slots, own, low, high, queries, weight, attn_out, keep_out, give_out, pred_out, window
):
    members, points, width = queries.shape
    half = width // 2
    here = core[0] == 0
    rows = window.shape[0]
    nodes, reach = own.shape[1], low.shape[1]
    share = pred_out.shape[2]
    window[nodes + 2 * reach :] = jnp.zeros((rows - nodes - 2 * reach, window.shape[1]), bf16)
    place = lax.broadcasted_iota(jnp.int32, (rows, points), 0)
    count = jnp.zeros((rows, points), f32)
    for slot in range(slots.shape[0]):
        count = count + (place == slots[slot : slot + 1]).astype(f32)
    used = count > 0.0
    for m in range(members):
        fill_window(window, m, own, low, high)
        scores = dot(window[...], queries[m], 1, 1) * scale
        scores = jnp.where(used, scores, -1e30)
        top = jnp.max(scores, axis=0, keepdims=True)
        raised = count * jnp.exp(scores - top)
        attn = raised / jnp.sum(raised, axis=0, keepdims=True)
        attn_out[m] = attn
        attn_high, attn_low = halves(attn)
        mixed = queries[m].astype(f32) + (
            dot(attn_high, window[...], 0, 0) + dot(attn_low, window[...], 0, 0)
        )
        mixed = mixed.astype(bf16)
        left, right = mixed[:, :half], mixed[:, half:]
        keep_out[m] = jnp.where(here, left, right)
        give_out[m] = jnp.where(here, right, left)
        pred = dot(mixed, weight[...], 1, 1)
        for k in range(points // share):
            pred_out[k, m] = pred[k * share : (k + 1) * share]


def crps_kernel(rows, target, weighting, out):
    groups, each, share, lanes = rows.shape
    count = groups * each
    eps_fair = (1.0 - fairness) / count
    values = [rows[k // each, k % each] for k in range(count)]
    spread = [jnp.zeros((share, lanes), f32) for _ in range(count)]
    for a in range(count):
        for b in range(a + 1, count):
            s = slope(values[a] - values[b])
            spread[a] = spread[a] + s
            spread[b] = spread[b] - s
    for k in range(count):
        skill = slope(values[k] - target[...])
        grad = weighting[...] * (
            skill / count - (1.0 - eps_fair) / (count * (count - 1)) * spread[k]
        )
        grad = grad.astype(bf16)
        group, m = k // each, k % each
        out[group, m] = grad
        out[group ^ 1, each + m] = grad


def weight_kernel(grads, keep, got, out):
    owners, _, share, lanes = grads.shape
    members = keep.shape[0]
    points = owners * share
    total = None
    for m in range(members):
        for part, mixed in ((m, keep), (members + m, got)):
            g = grads[:, part].reshape(points, lanes)
            term = dot(g, mixed[m], 0, 0)
            total = term if total is None else total + term
    pieces, high, wide = out.shape
    across = total.shape[1] // wide
    for k in range(pieces):
        r, c = k // across * high, k % across * wide
        out[k] = total[r : r + high, c : c + wide].astype(bf16)


def add_kernel(terms, out):
    total = terms[0].astype(f32)
    for k in range(1, terms.shape[0]):
        total = total + terms[k].astype(f32)
    total = total.astype(bf16)
    for k in range(out.shape[0]):
        out[k] = total


def assemble_kernel(core, mine, other, out):
    pieces, high, wide = mine.shape
    half = out.shape[1] // 2
    across = half // wide
    here = core[0] == 0
    for k in range(pieces):
        r, c = k // across * high, k % across * wide
        size = min(high, out.shape[0] - r)
        if size > 0:
            a, b = mine[k].astype(f32)[:size], other[k].astype(f32)[:size]
            out[r : r + size, c : c + wide] = jnp.where(here, a, b)
            out[r : r + size, half + c : half + c + wide] = jnp.where(here, b, a)


def backward_kernel(
    scale, grads, attn, own, low, high, queries, weight, own_out, low_out, high_out, window
):
    owners, _, share, lanes = grads.shape
    members = queries.shape[0]
    points = owners * share
    rows = window.shape[0]
    nodes, reach = own.shape[1], low.shape[1]
    window[nodes + 2 * reach :] = jnp.zeros((rows - nodes - 2 * reach, window.shape[1]), bf16)
    for m in range(members):
        fill_window(window, m, own, low, high)
        g = grads[:, m].reshape(points, lanes)
        dmixed = dot(g, weight[...], 1, 0).astype(bf16)
        dattn = dot(window[...], dmixed, 1, 1)
        a = attn[m]
        dscores = a * (dattn - jnp.sum(a * dattn, axis=0, keepdims=True)) * scale
        a_high, a_low = halves(a)
        s_high, s_low = halves(dscores)
        total = (
            dot(a_high, dmixed, 1, 0)
            + dot(s_high, queries[m], 1, 0)
            + dot(a_low, dmixed, 1, 0)
            + dot(s_low, queries[m], 1, 0)
        )
        own_out[m] = total[:nodes]
        low_out[m] = total[nodes : nodes + reach].astype(bf16)
        high_out[m] = total[nodes + reach : nodes + 2 * reach].astype(bf16)


def finish_kernel(own, from_prev, from_next, out):
    nodes, reach = own.shape[1], from_prev.shape[1]
    for m in range(own.shape[0]):
        out[m, :reach] = (own[m, :reach] + from_prev[m].astype(f32)).astype(bf16)
        out[m, reach : nodes - reach] = own[m, reach : nodes - reach].astype(bf16)
        out[m, nodes - reach :] = (own[m, nodes - reach :] + from_next[m].astype(f32)).astype(bf16)


def call(kernel, out_shape, args, scratch=(), name=None, scalars=0):
    vmem, smem = pl.BlockSpec(memory_space=pltpu.VMEM), pl.BlockSpec(memory_space=pltpu.SMEM)
    single = not isinstance(out_shape, (list, tuple))
    return pl.pallas_call(
        kernel,
        out_shape=out_shape,
        in_specs=[smem] * scalars + [vmem] * (len(args) - scalars),
        out_specs=vmem if single else [vmem] * len(out_shape),
        scratch_shapes=list(scratch),
        compiler_params=pltpu.CompilerParams(vmem_limit_bytes=VMEM_LIMIT),
        name=name,
    )(*args)


def add_up(terms, copies, name):
    return call(add_kernel, jax.ShapeDtypeStruct((copies,) + terms.shape[1:], bf16), (terms,), name=name)


def exchange(x, axes):
    return lax.all_to_all(x, axes, 0, 0, tiled=True)


def local(latents, queries, neighbours, truth, area_weight, var_weight, proj_weight):
    members, nodes, width = latents.shape
    points = queries.shape[1]
    variables = proj_weight.shape[1]
    reach = nodes // 4
    scale = 1.0 / math.sqrt(width)
    shards = lax.axis_size(SHARD)
    owners = lax.axis_size(MEMBER)
    share = points // owners
    forward = [(i, (i + 1) % shards) for i in range(shards)]
    backward = [(i, (i - 1) % shards) for i in range(shards)]

    low = lax.ppermute(latents[:, nodes - reach :], SHARD, forward)
    high = lax.ppermute(latents[:, :reach], SHARD, backward)

    first = lax.axis_index(SHARD) * nodes
    index = (neighbours.T - first + reach) % (nodes * shards)
    slots = jnp.where(
        index < reach, index + nodes, jnp.where(index < nodes + reach, index - reach, index)
    )
    weight = jnp.pad(proj_weight.T, ((0, LANES - variables), (0, 0)))
    start = lax.axis_index(MEMBER) * share
    pad_lanes = ((0, 0), (0, LANES - variables))
    target = jnp.pad(lax.dynamic_slice_in_dim(truth, start, share, 0), pad_lanes)
    area = lax.dynamic_slice_in_dim(area_weight, start, share, 0)
    weighting = jnp.pad(area[:, None] * var_weight[None, :], pad_lanes)

    window_rows = 2 * LANES
    window = pltpu.VMEM((window_rows, width), bf16)
    core = lax.axis_index("core").astype(jnp.int32).reshape(1)
    swap = [(0, 1), (1, 0)]
    attn, keep, give, pred = call(
        functools.partial(forward_kernel, scale),
        [
            jax.ShapeDtypeStruct((members, window_rows, points), f32),
            jax.ShapeDtypeStruct((members, points, width // 2), bf16),
            jax.ShapeDtypeStruct((members, points, width // 2), bf16),
            jax.ShapeDtypeStruct((owners, members, share, LANES), f32),
        ],
        (core, slots, latents, low, high, queries, weight),
        [window],
        name="forward",
        scalars=1,
    )
    rows = exchange(pred, MEMBER)
    got = lax.ppermute(give, "core", swap)
    owner_grad = call(
        crps_kernel,
        jax.ShapeDtypeStruct((owners, 2 * members, share, LANES), bf16),
        (rows, target, weighting),
        name="crps",
    )
    grads = exchange(owner_grad, MEMBER)

    pieces = lax.axis_size(SPREAD)
    tall = width // 2 // pieces
    term = call(
        weight_kernel,
        jax.ShapeDtypeStruct((pieces, tall, LANES), bf16),
        (grads, keep, got),
        name="weight_term",
    )
    term = exchange(term, SPREAD)

    own_part, low_part, high_part = call(
        functools.partial(backward_kernel, scale),
        [
            jax.ShapeDtypeStruct((members, nodes, width), f32),
            jax.ShapeDtypeStruct((members, reach, width), bf16),
            jax.ShapeDtypeStruct((members, reach, width), bf16),
        ],
        (grads, attn, latents, low, high, queries, weight),
        [window],
        name="backward",
    )
    term, low_part, high_part = lax.optimization_barrier((term, low_part, high_part))
    from_next = lax.ppermute(low_part, SHARD, backward)
    from_prev = lax.ppermute(high_part, SHARD, forward)
    piece = exchange(add_up(term, lax.axis_size("z"), "add_plane"), "z")
    mine = exchange(add_up(piece, pieces, "add_z"), SPREAD)
    other = lax.ppermute(mine, "core", swap)
    proj_grad = call(
        assemble_kernel,
        jax.ShapeDtypeStruct((variables, width), f32),
        (core, mine, other),
        name="assemble",
        scalars=1,
    ).T

    latent_grad = call(
        finish_kernel,
        jax.ShapeDtypeStruct(latents.shape, bf16),
        (own_part, from_prev, from_next),
        name="finish",
    )
    return latent_grad, proj_grad


def solution(mesh):
    fine = Mesh(mesh.devices.reshape(4, 2, 12, 4, 2), MEMBER + SHARD)
    placed = (
        P(MEMBER, SHARD, None),
        P(MEMBER, SHARD, None),
        P(SHARD, None),
        P(SHARD, None),
        P(SHARD),
        P(),
        P(),
    )
    return jax.shard_map(
        local,
        mesh=fine,
        in_specs=placed,
        out_specs=(P(MEMBER, SHARD, None), P()),
        check_vma=False,
    )
```

```python
import functools
import math

import jax
import jax.numpy as jnp
from jax import lax
from jax.experimental import pallas as pl
from jax.experimental.pallas import tpu as pltpu
from jax.sharding import Mesh, PartitionSpec as P

smoothing = 0.25
fairness = 0.95
LANES = 128
f32, bf16 = jnp.float32, jnp.bfloat16

MEMBER = ("ylo", "core")
SHARD = ("z", "x", "yhi")
SPREAD = ("x", "ylo", "yhi")
VMEM_LIMIT = 48 * 1024 * 1024


def slope(diff):
    return diff * lax.rsqrt(diff * diff + smoothing * smoothing)


def dot(a, b, ca, cb):
    return lax.dot_general(a, b, (((ca,), (cb,)), ((), ())), preferred_element_type=f32)


def halves(x):
    high = x.astype(bf16)
    return high, (x - high.astype(f32)).astype(bf16)


def fill_window(window, m, own, low, high):
    nodes, reach = own.shape[1], low.shape[1]
    window[0:nodes] = own[m]
    window[nodes : nodes + reach] = low[m]
    window[nodes + reach : nodes + 2 * reach] = high[m]


def forward_kernel(
    scale, core, slots, own, low, high, queries, weight, attn_out, keep_out, give_out, pred_out, window
):
    members, points, width = queries.shape
    half = width // 2
    here = core[0] == 0
    rows = window.shape[0]
    nodes, reach = own.shape[1], low.shape[1]
    share = pred_out.shape[2]
    window[nodes + 2 * reach :] = jnp.zeros((rows - nodes - 2 * reach, window.shape[1]), bf16)
    place = lax.broadcasted_iota(jnp.int32, (rows, points), 0)
    count = jnp.zeros((rows, points), f32)
    for slot in range(slots.shape[0]):
        count = count + (place == slots[slot : slot + 1]).astype(f32)
    used = count > 0.0
    for m in range(members):
        fill_window(window, m, own, low, high)
        scores = dot(window[...], queries[m], 1, 1) * scale
        scores = jnp.where(used, scores, -1e30)
        top = jnp.max(scores, axis=0, keepdims=True)
        raised = count * jnp.exp(scores - top)
        attn = raised / jnp.sum(raised, axis=0, keepdims=True)
        attn_out[m] = attn
        attn_high, attn_low = halves(attn)
        mixed = queries[m].astype(f32) + (
            dot(attn_high, window[...], 0, 0) + dot(attn_low, window[...], 0, 0)
        )
        mixed = mixed.astype(bf16)
        left, right = mixed[:, :half], mixed[:, half:]
        keep_out[m] = jnp.where(here, left, right)
        give_out[m] = jnp.where(here, right, left)
        pred = dot(mixed, weight[...], 1, 1)
        for k in range(points // share):
            pred_out[k, m] = pred[k * share : (k + 1) * share]


def crps_kernel(rows, target, weighting, out):
    groups, each, share, lanes = rows.shape
    count = groups * each
    eps_fair = (1.0 - fairness) / count
    values = [rows[k // each, k % each] for k in range(count)]
    spread = [jnp.zeros((share, lanes), f32) for _ in range(count)]
    for a in range(count):
        for b in range(a + 1, count):
            s = slope(values[a] - values[b])
            spread[a] = spread[a] + s
            spread[b] = spread[b] - s
    for k in range(count):
        skill = slope(values[k] - target[...])
        grad = weighting[...] * (
            skill / count - (1.0 - eps_fair) / (count * (count - 1)) * spread[k]
        )
        grad = grad.astype(bf16)
        group, m = k // each, k % each
        out[group, m] = grad
        out[group ^ 1, each + m] = grad


def weight_kernel(grads, keep, got, out):
    owners, _, share, lanes = grads.shape
    members = keep.shape[0]
    points = owners * share
    total = None
    for m in range(members):
        for part, mixed in ((m, keep), (members + m, got)):
            g = grads[:, part].reshape(points, lanes)
            term = dot(g, mixed[m], 0, 0)
            total = term if total is None else total + term
    pieces, high, wide = out.shape
    across = total.shape[1] // wide
    for k in range(pieces):
        r, c = k // across * high, k % across * wide
        out[k] = total[r : r + high, c : c + wide].astype(bf16)


def add_kernel(terms, out):
    total = terms[0].astype(f32)
    for k in range(1, terms.shape[0]):
        total = total + terms[k].astype(f32)
    total = total.astype(bf16)
    for k in range(out.shape[0]):
        out[k] = total


def assemble_kernel(core, mine, other, out):
    pieces, high, wide = mine.shape
    half = out.shape[1] // 2
    across = half // wide
    here = core[0] == 0
    for k in range(pieces):
        r, c = k // across * high, k % across * wide
        size = min(high, out.shape[0] - r)
        if size > 0:
            a, b = mine[k].astype(f32)[:size], other[k].astype(f32)[:size]
            out[r : r + size, c : c + wide] = jnp.where(here, a, b)
            out[r : r + size, half + c : half + c + wide] = jnp.where(here, b, a)


def backward_kernel(
    scale, grads, attn, own, low, high, queries, weight, own_out, low_out, high_out, window
):
    owners, _, share, lanes = grads.shape
    members = queries.shape[0]
    points = owners * share
    rows = window.shape[0]
    nodes, reach = own.shape[1], low.shape[1]
    window[nodes + 2 * reach :] = jnp.zeros((rows - nodes - 2 * reach, window.shape[1]), bf16)
    for m in range(members):
        fill_window(window, m, own, low, high)
        g = grads[:, m].reshape(points, lanes)
        dmixed = dot(g, weight[...], 1, 0).astype(bf16)
        dattn = dot(window[...], dmixed, 1, 1)
        a = attn[m]
        dscores = a * (dattn - jnp.sum(a * dattn, axis=0, keepdims=True)) * scale
        a_high, a_low = halves(a)
        s_high, s_low = halves(dscores)
        total = (
            dot(a_high, dmixed, 1, 0)
            + dot(s_high, queries[m], 1, 0)
            + dot(a_low, dmixed, 1, 0)
            + dot(s_low, queries[m], 1, 0)
        )
        own_out[m] = total[:nodes]
        low_out[m] = total[nodes : nodes + reach].astype(bf16)
        high_out[m] = total[nodes + reach : nodes + 2 * reach].astype(bf16)


def finish_kernel(own, from_prev, from_next, out):
    nodes, reach = own.shape[1], from_prev.shape[1]
    for m in range(own.shape[0]):
        out[m, :reach] = (own[m, :reach] + from_prev[m].astype(f32)).astype(bf16)
        out[m, reach : nodes - reach] = own[m, reach : nodes - reach].astype(bf16)
        out[m, nodes - reach :] = (own[m, nodes - reach :] + from_next[m].astype(f32)).astype(bf16)


def call(kernel, out_shape, args, scratch=(), name=None, scalars=0):
    vmem, smem = pl.BlockSpec(memory_space=pltpu.VMEM), pl.BlockSpec(memory_space=pltpu.SMEM)
    single = not isinstance(out_shape, (list, tuple))
    return pl.pallas_call(
        kernel,
        out_shape=out_shape,
        in_specs=[smem] * scalars + [vmem] * (len(args) - scalars),
        out_specs=vmem if single else [vmem] * len(out_shape),
        scratch_shapes=list(scratch),
        compiler_params=pltpu.CompilerParams(vmem_limit_bytes=VMEM_LIMIT),
        name=name,
    )(*args)


def add_up(terms, copies, name):
    return call(add_kernel, jax.ShapeDtypeStruct((copies,) + terms.shape[1:], bf16), (terms,), name=name)


def exchange(x, axes):
    return lax.all_to_all(x, axes, 0, 0, tiled=True)


def whole_exchange(x):
    return exchange(x, SPREAD)


def split_exchange(x):
    x = x.reshape((lax.axis_size(SPREAD[0]), -1) + x.shape[1:])
    x = exchange(x, SPREAD[:1])
    return lax.all_to_all(x, SPREAD[1:], 1, 1, tiled=True).reshape((-1,) + x.shape[2:])


def local(latents, queries, neighbours, truth, area_weight, var_weight, proj_weight):
    members, nodes, width = latents.shape
    points = queries.shape[1]
    variables = proj_weight.shape[1]
    reach = nodes // 4
    scale = 1.0 / math.sqrt(width)
    shards = lax.axis_size(SHARD)
    owners = lax.axis_size(MEMBER)
    share = points // owners
    forward = [(i, (i + 1) % shards) for i in range(shards)]
    backward = [(i, (i - 1) % shards) for i in range(shards)]

    low = lax.ppermute(latents[:, nodes - reach :], SHARD, forward)
    high = lax.ppermute(latents[:, :reach], SHARD, backward)

    first = lax.axis_index(SHARD) * nodes
    index = (neighbours.T - first + reach) % (nodes * shards)
    slots = jnp.where(
        index < reach, index + nodes, jnp.where(index < nodes + reach, index - reach, index)
    )
    weight = jnp.pad(proj_weight.T, ((0, LANES - variables), (0, 0)))
    start = lax.axis_index(MEMBER) * share
    pad_lanes = ((0, 0), (0, LANES - variables))
    target = jnp.pad(lax.dynamic_slice_in_dim(truth, start, share, 0), pad_lanes)
    area = lax.dynamic_slice_in_dim(area_weight, start, share, 0)
    weighting = jnp.pad(area[:, None] * var_weight[None, :], pad_lanes)

    window_rows = 2 * LANES
    window = pltpu.VMEM((window_rows, width), bf16)
    core = lax.axis_index("core").astype(jnp.int32).reshape(1)
    swap = [(0, 1), (1, 0)]
    attn, keep, give, pred = call(
        functools.partial(forward_kernel, scale),
        [
            jax.ShapeDtypeStruct((members, window_rows, points), f32),
            jax.ShapeDtypeStruct((members, points, width // 2), bf16),
            jax.ShapeDtypeStruct((members, points, width // 2), bf16),
            jax.ShapeDtypeStruct((owners, members, share, LANES), f32),
        ],
        (core, slots, latents, low, high, queries, weight),
        [window],
        name="forward",
        scalars=1,
    )
    rows = exchange(pred, MEMBER)
    got = lax.ppermute(give, "core", swap)
    owner_grad = call(
        crps_kernel,
        jax.ShapeDtypeStruct((owners, 2 * members, share, LANES), bf16),
        (rows, target, weighting),
        name="crps",
    )
    grads = exchange(owner_grad, MEMBER)

    pieces = lax.axis_size(SPREAD)
    tall = width // 2 // pieces
    term = call(
        weight_kernel,
        jax.ShapeDtypeStruct((pieces, tall, LANES), bf16),
        (grads, keep, got),
        name="weight_term",
    )
    term = exchange(term, SPREAD)

    own_part, low_part, high_part = call(
        functools.partial(backward_kernel, scale),
        [
            jax.ShapeDtypeStruct((members, nodes, width), f32),
            jax.ShapeDtypeStruct((members, reach, width), bf16),
            jax.ShapeDtypeStruct((members, reach, width), bf16),
        ],
        (grads, attn, latents, low, high, queries, weight),
        [window],
        name="backward",
    )
    term, low_part, high_part = lax.optimization_barrier((term, low_part, high_part))
    from_next = lax.ppermute(low_part, SHARD, backward)
    from_prev = lax.ppermute(high_part, SHARD, forward)
    piece = exchange(add_up(term, lax.axis_size("z"), "add_plane"), "z")
    mine = lax.cond(var_weight[0] > 0.0, whole_exchange, split_exchange, add_up(piece, pieces, "add_z"))
    other = lax.ppermute(mine, "core", swap)
    proj_grad = call(
        assemble_kernel,
        jax.ShapeDtypeStruct((variables, width), f32),
        (core, mine, other),
        name="assemble",
        scalars=1,
    ).T

    latent_grad = call(
        finish_kernel,
        jax.ShapeDtypeStruct(latents.shape, bf16),
        (own_part, from_prev, from_next),
        name="finish",
    )
    return latent_grad, proj_grad


def solution(mesh):
    fine = Mesh(mesh.devices.reshape(4, 2, 12, 4, 2), MEMBER + SHARD)
    placed = (
        P(MEMBER, SHARD, None),
        P(MEMBER, SHARD, None),
        P(SHARD, None),
        P(SHARD, None),
        P(SHARD),
        P(),
        P(),
    )
    return jax.shard_map(
        local,
        mesh=fine,
        in_specs=placed,
        out_specs=(P(MEMBER, SHARD, None), P()),
        check_vma=False,
    )
```

```python
import functools
import math

import jax
import jax.numpy as jnp
from jax import lax
from jax.experimental import pallas as pl
from jax.experimental.pallas import tpu as pltpu
from jax.sharding import Mesh, PartitionSpec as P

smoothing = 0.25
fairness = 0.95
LANES = 128
f32, bf16 = jnp.float32, jnp.bfloat16

MEMBER = ("ylo", "core")
SHARD = ("z", "x", "yhi")
SPREAD = ("x", "ylo", "yhi")
VMEM_LIMIT = 48 * 1024 * 1024


def slope(diff):
    return diff * lax.rsqrt(diff * diff + smoothing * smoothing)


def dot(a, b, ca, cb):
    return lax.dot_general(a, b, (((ca,), (cb,)), ((), ())), preferred_element_type=f32)


def halves(x):
    high = x.astype(bf16)
    return high, (x - high.astype(f32)).astype(bf16)


def fill_window(window, m, own, low, high):
    nodes, reach = own.shape[1], low.shape[1]
    window[0:nodes] = own[m]
    window[nodes : nodes + reach] = low[m]
    window[nodes + reach : nodes + 2 * reach] = high[m]


def prepare_kernel(slots, own, queries, count_out, scores_out):
    rows, points = count_out.shape
    place = lax.broadcasted_iota(jnp.int32, (rows, points), 0)
    count = jnp.zeros((rows, points), f32)
    for slot in range(slots.shape[0]):
        count = count + (place == slots[slot : slot + 1]).astype(f32)
    count_out[...] = count
    for m in range(queries.shape[0]):
        scores_out[m] = dot(own[m], queries[m], 1, 1)


def forward_kernel(
    scale, core, counts, near, own, low, high, queries, weight,
    attn_out, keep_out, give_out, pred_out, window,
):
    members, points, width = queries.shape
    half = width // 2
    here = core[0] == 0
    nodes = own.shape[1]
    share = pred_out.shape[2]
    count = counts[...]
    used = count > 0.0
    for m in range(members):
        fill_window(window, m, own, low, high)
        scores = jnp.concatenate([near[m], dot(window[nodes:], queries[m], 1, 1)]) * scale
        scores = jnp.where(used, scores, -1e30)
        top = jnp.max(scores, axis=0, keepdims=True)
        raised = count * jnp.exp(scores - top)
        attn = raised / jnp.sum(raised, axis=0, keepdims=True)
        attn_out[m] = attn
        attn_high, attn_low = halves(attn)
        mixed = queries[m].astype(f32) + (
            dot(attn_high, window[...], 0, 0) + dot(attn_low, window[...], 0, 0)
        )
        mixed = mixed.astype(bf16)
        left, right = mixed[:, :half], mixed[:, half:]
        keep_out[m] = jnp.where(here, left, right)
        give_out[m] = jnp.where(here, right, left)
        pred = dot(mixed, weight[...], 1, 1)
        for k in range(points // share):
            pred_out[k, m] = pred[k * share : (k + 1) * share]


def crps_kernel(rows, target, weighting, out):
    groups, each, share, lanes = rows.shape
    count = groups * each
    eps_fair = (1.0 - fairness) / count
    values = [rows[k // each, k % each] for k in range(count)]
    spread = [jnp.zeros((share, lanes), f32) for _ in range(count)]
    for a in range(count):
        for b in range(a + 1, count):
            s = slope(values[a] - values[b])
            spread[a] = spread[a] + s
            spread[b] = spread[b] - s
    for k in range(count):
        skill = slope(values[k] - target[...])
        grad = weighting[...] * (
            skill / count - (1.0 - eps_fair) / (count * (count - 1)) * spread[k]
        )
        grad = grad.astype(bf16)
        group, m = k // each, k % each
        out[group, m] = grad
        out[group ^ 1, each + m] = grad


def weight_kernel(grads, keep, got, out):
    owners, _, share, lanes = grads.shape
    members = keep.shape[0]
    points = owners * share
    total = None
    for m in range(members):
        for part, mixed in ((m, keep), (members + m, got)):
            g = grads[:, part].reshape(points, lanes)
            term = dot(g, mixed[m], 0, 0)
            total = term if total is None else total + term
    pieces, high, wide = out.shape
    across = total.shape[1] // wide
    for k in range(pieces):
        r, c = k // across * high, k % across * wide
        out[k] = total[r : r + high, c : c + wide].astype(bf16)


def add_kernel(terms, out):
    total = terms[0].astype(f32)
    for k in range(1, terms.shape[0]):
        total = total + terms[k].astype(f32)
    total = total.astype(bf16)
    for k in range(out.shape[0]):
        out[k] = total


def assemble_kernel(core, mine, other, out):
    pieces, high, wide = mine.shape
    half = out.shape[1] // 2
    across = half // wide
    here = core[0] == 0
    for k in range(pieces):
        r, c = k // across * high, k % across * wide
        size = min(high, out.shape[0] - r)
        if size > 0:
            a, b = mine[k].astype(f32)[:size], other[k].astype(f32)[:size]
            out[r : r + size, c : c + wide] = jnp.where(here, a, b)
            out[r : r + size, half + c : half + c + wide] = jnp.where(here, b, a)


def backward_kernel(
    scale, grads, attn, own, low, high, queries, weight, own_out, low_out, high_out, window
):
    owners, _, share, lanes = grads.shape
    members = queries.shape[0]
    points = owners * share
    nodes, reach = own.shape[1], low.shape[1]
    for m in range(members):
        fill_window(window, m, own, low, high)
        g = grads[:, m].reshape(points, lanes)
        dmixed = dot(g, weight[...], 1, 0).astype(bf16)
        dattn = dot(window[...], dmixed, 1, 1)
        a = attn[m]
        dscores = a * (dattn - jnp.sum(a * dattn, axis=0, keepdims=True)) * scale
        a_high, a_low = halves(a)
        s_high, s_low = halves(dscores)
        total = (
            dot(a_high, dmixed, 1, 0)
            + dot(s_high, queries[m], 1, 0)
            + dot(a_low, dmixed, 1, 0)
            + dot(s_low, queries[m], 1, 0)
        )
        own_out[m] = total[:nodes]
        low_out[m] = total[nodes : nodes + reach].astype(bf16)
        high_out[m] = total[nodes + reach : nodes + 2 * reach].astype(bf16)


def finish_kernel(own, from_prev, from_next, out):
    nodes, reach = own.shape[1], from_prev.shape[1]
    for m in range(own.shape[0]):
        out[m, :reach] = (own[m, :reach] + from_prev[m].astype(f32)).astype(bf16)
        out[m, reach : nodes - reach] = own[m, reach : nodes - reach].astype(bf16)
        out[m, nodes - reach :] = (own[m, nodes - reach :] + from_next[m].astype(f32)).astype(bf16)


def call(kernel, out_shape, args, scratch=(), name=None, scalars=0):
    vmem, smem = pl.BlockSpec(memory_space=pltpu.VMEM), pl.BlockSpec(memory_space=pltpu.SMEM)
    single = not isinstance(out_shape, (list, tuple))
    return pl.pallas_call(
        kernel,
        out_shape=out_shape,
        in_specs=[smem] * scalars + [vmem] * (len(args) - scalars),
        out_specs=vmem if single else [vmem] * len(out_shape),
        scratch_shapes=list(scratch),
        compiler_params=pltpu.CompilerParams(vmem_limit_bytes=VMEM_LIMIT),
        name=name,
    )(*args)


def add_up(terms, copies, name):
    return call(add_kernel, jax.ShapeDtypeStruct((copies,) + terms.shape[1:], bf16), (terms,), name=name)


def exchange(x, axes):
    return lax.all_to_all(x, axes, 0, 0, tiled=True)


def whole_exchange(x):
    return exchange(x, SPREAD)


def split_exchange(x):
    x = x.reshape((lax.axis_size(SPREAD[0]), -1) + x.shape[1:])
    x = exchange(x, SPREAD[:1])
    return lax.all_to_all(x, SPREAD[1:], 1, 1, tiled=True).reshape((-1,) + x.shape[2:])


def local(latents, queries, neighbours, truth, area_weight, var_weight, proj_weight):
    members, nodes, width = latents.shape
    points = queries.shape[1]
    variables = proj_weight.shape[1]
    reach = nodes // 4
    scale = 1.0 / math.sqrt(width)
    shards = lax.axis_size(SHARD)
    owners = lax.axis_size(MEMBER)
    share = points // owners
    forward = [(i, (i + 1) % shards) for i in range(shards)]
    backward = [(i, (i - 1) % shards) for i in range(shards)]

    low = lax.ppermute(latents[:, nodes - reach :], SHARD, forward)
    high = lax.ppermute(latents[:, :reach], SHARD, backward)

    first = lax.axis_index(SHARD) * nodes
    index = (neighbours.T - first + reach) % (nodes * shards)
    slots = jnp.where(
        index < reach, index + nodes, jnp.where(index < nodes + reach, index - reach, index)
    )
    weight = jnp.pad(proj_weight.T, ((0, LANES - variables), (0, 0)))
    start = lax.axis_index(MEMBER) * share
    pad_lanes = ((0, 0), (0, LANES - variables))
    target = jnp.pad(lax.dynamic_slice_in_dim(truth, start, share, 0), pad_lanes)
    area = lax.dynamic_slice_in_dim(area_weight, start, share, 0)
    weighting = jnp.pad(area[:, None] * var_weight[None, :], pad_lanes)

    window_rows = nodes + 2 * reach
    window = pltpu.VMEM((window_rows, width), bf16)
    core = lax.axis_index("core").astype(jnp.int32).reshape(1)
    swap = [(0, 1), (1, 0)]
    counts, near = call(
        prepare_kernel,
        [
            jax.ShapeDtypeStruct((window_rows, points), f32),
            jax.ShapeDtypeStruct((members, nodes, points), f32),
        ],
        (slots, latents, queries),
        name="prepare",
    )
    attn, keep, give, pred = call(
        functools.partial(forward_kernel, scale),
        [
            jax.ShapeDtypeStruct((members, window_rows, points), f32),
            jax.ShapeDtypeStruct((members, points, width // 2), bf16),
            jax.ShapeDtypeStruct((members, points, width // 2), bf16),
            jax.ShapeDtypeStruct((owners, members, share, LANES), f32),
        ],
        (core, counts, near, latents, low, high, queries, weight),
        [window],
        name="forward",
        scalars=1,
    )
    rows = exchange(pred, MEMBER)
    got = lax.ppermute(give, "core", swap)
    owner_grad = call(
        crps_kernel,
        jax.ShapeDtypeStruct((owners, 2 * members, share, LANES), bf16),
        (rows, target, weighting),
        name="crps",
    )
    grads = exchange(owner_grad, MEMBER)

    pieces = lax.axis_size(SPREAD)
    tall = width // 2 // pieces
    term = call(
        weight_kernel,
        jax.ShapeDtypeStruct((pieces, tall, LANES), bf16),
        (grads, keep, got),
        name="weight_term",
    )
    term = exchange(term, SPREAD)

    own_part, low_part, high_part = call(
        functools.partial(backward_kernel, scale),
        [
            jax.ShapeDtypeStruct((members, nodes, width), f32),
            jax.ShapeDtypeStruct((members, reach, width), bf16),
            jax.ShapeDtypeStruct((members, reach, width), bf16),
        ],
        (grads, attn, latents, low, high, queries, weight),
        [window],
        name="backward",
    )
    term, low_part, high_part = lax.optimization_barrier((term, low_part, high_part))
    from_next = lax.ppermute(low_part, SHARD, backward)
    from_prev = lax.ppermute(high_part, SHARD, forward)
    piece = exchange(add_up(term, lax.axis_size("z"), "add_plane"), "z")
    mine = lax.cond(var_weight[0] > 0.0, whole_exchange, split_exchange, add_up(piece, pieces, "add_z"))
    other = lax.ppermute(mine, "core", swap)
    proj_grad = call(
        assemble_kernel,
        jax.ShapeDtypeStruct((variables, width), f32),
        (core, mine, other),
        name="assemble",
        scalars=1,
    ).T

    latent_grad = call(
        finish_kernel,
        jax.ShapeDtypeStruct(latents.shape, bf16),
        (own_part, from_prev, from_next),
        name="finish",
    )
    return latent_grad, proj_grad


def solution(mesh):
    fine = Mesh(mesh.devices.reshape(4, 2, 12, 4, 2), MEMBER + SHARD)
    placed = (
        P(MEMBER, SHARD, None),
        P(MEMBER, SHARD, None),
        P(SHARD, None),
        P(SHARD, None),
        P(SHARD),
        P(),
        P(),
    )
    return jax.shard_map(
        local,
        mesh=fine,
        in_specs=placed,
        out_specs=(P(MEMBER, SHARD, None), P()),
        check_vma=False,
    )
```

```python
import functools
import math

import jax
import jax.numpy as jnp
from jax import lax
from jax.experimental import pallas as pl
from jax.experimental.pallas import tpu as pltpu
from jax.sharding import Mesh, PartitionSpec as P

smoothing = 0.25
fairness = 0.95
LANES = 128
f32, bf16 = jnp.float32, jnp.bfloat16

MEMBER = ("ylo", "core")
SHARD = ("z", "x", "yhi")
SPREAD = ("x", "ylo", "yhi")
VMEM_LIMIT = 48 * 1024 * 1024


def slope(diff):
    return diff * lax.rsqrt(diff * diff + smoothing * smoothing)


def dot(a, b, ca, cb):
    return lax.dot_general(a, b, (((ca,), (cb,)), ((), ())), preferred_element_type=f32)


def halves(x):
    high = x.astype(bf16)
    return high, (x - high.astype(f32)).astype(bf16)


def fill_window(window, m, own, low, high):
    nodes, reach = own.shape[1], low.shape[1]
    window[0:nodes] = own[m]
    window[nodes : nodes + reach] = low[m]
    window[nodes + reach : nodes + 2 * reach] = high[m]


def prepare_kernel(slots, own, queries, count_out, scores_out):
    rows, points = count_out.shape
    place = lax.broadcasted_iota(jnp.int32, (rows, points), 0)
    count = jnp.zeros((rows, points), f32)
    for slot in range(slots.shape[0]):
        count = count + (place == slots[slot : slot + 1]).astype(f32)
    count_out[...] = count
    for m in range(queries.shape[0]):
        scores_out[m] = dot(own[m], queries[m], 1, 1)


def forward_kernel(
    scale, core, counts, near, own, low, high, queries, weight,
    attn_out, keep_out, give_out, pred_out, window,
):
    members, points, width = queries.shape
    half = width // 2
    here = core[0] == 0
    nodes = own.shape[1]
    share = pred_out.shape[2]
    count = counts[...]
    used = count > 0.0
    for m in range(members):
        fill_window(window, m, own, low, high)
        scores = jnp.concatenate([near[m], dot(window[nodes:], queries[m], 1, 1)]) * scale
        scores = jnp.where(used, scores, -1e30)
        top = jnp.max(scores, axis=0, keepdims=True)
        raised = count * jnp.exp(scores - top)
        attn = raised / jnp.sum(raised, axis=0, keepdims=True)
        attn_out[m] = attn
        attn_high, attn_low = halves(attn)
        mixed = queries[m].astype(f32) + (
            dot(attn_high, window[...], 0, 0) + dot(attn_low, window[...], 0, 0)
        )
        mixed = mixed.astype(bf16)
        left, right = mixed[:, :half], mixed[:, half:]
        keep_out[m] = jnp.where(here, left, right)
        give_out[m] = jnp.where(here, right, left)
        pred = dot(mixed, weight[...], 1, 1)
        for k in range(points // share):
            pred_out[k, m] = pred[k * share : (k + 1) * share]


def crps_kernel(rows, target, weighting, out):
    groups, each, share, lanes = rows.shape
    count = groups * each
    eps_fair = (1.0 - fairness) / count
    values = [rows[k // each, k % each] for k in range(count)]
    spread = [jnp.zeros((share, lanes), f32) for _ in range(count)]
    for a in range(count):
        for b in range(a + 1, count):
            s = slope(values[a] - values[b])
            spread[a] = spread[a] + s
            spread[b] = spread[b] - s
    for k in range(count):
        skill = slope(values[k] - target[...])
        grad = weighting[...] * (
            skill / count - (1.0 - eps_fair) / (count * (count - 1)) * spread[k]
        )
        grad = grad.astype(bf16)
        group, m = k // each, k % each
        out[group, m] = grad
        out[group ^ 1, each + m] = grad


def weight_kernel(grads, keep, got, out):
    owners, _, share, lanes = grads.shape
    members = keep.shape[0]
    points = owners * share
    total = None
    for m in range(members):
        for part, mixed in ((m, keep), (members + m, got)):
            g = grads[:, part].reshape(points, lanes)
            term = dot(g, mixed[m], 0, 0)
            total = term if total is None else total + term
    pieces, high, wide = out.shape
    across = total.shape[1] // wide
    for k in range(pieces):
        r, c = k // across * high, k % across * wide
        out[k] = total[r : r + high, c : c + wide].astype(bf16)


def add_kernel(terms, out):
    total = terms[0].astype(f32)
    for k in range(1, terms.shape[0]):
        total = total + terms[k].astype(f32)
    total = total.astype(bf16)
    for k in range(out.shape[0]):
        out[k] = total


def assemble_kernel(core, mine, other, out):
    pieces, high, wide = mine.shape
    half = out.shape[1] // 2
    across = half // wide
    here = core[0] == 0
    for k in range(pieces):
        r, c = k // across * high, k % across * wide
        size = min(high, out.shape[0] - r)
        if size > 0:
            a, b = mine[k].astype(f32)[:size], other[k].astype(f32)[:size]
            out[r : r + size, c : c + wide] = jnp.where(here, a, b)
            out[r : r + size, half + c : half + c + wide] = jnp.where(here, b, a)


def backward_kernel(
    scale, side, grads, attn, own, low, high, queries, weight, own_out, even_out, odd_out, window
):
    first = side[0] == 0
    owners, _, share, lanes = grads.shape
    members = queries.shape[0]
    points = owners * share
    nodes, reach = own.shape[1], low.shape[1]
    for m in range(members):
        fill_window(window, m, own, low, high)
        g = grads[:, m].reshape(points, lanes)
        dmixed = dot(g, weight[...], 1, 0).astype(bf16)
        dattn = dot(window[...], dmixed, 1, 1)
        a = attn[m]
        dscores = a * (dattn - jnp.sum(a * dattn, axis=0, keepdims=True)) * scale
        a_high, a_low = halves(a)
        s_high, s_low = halves(dscores)
        total = (
            dot(a_high, dmixed, 1, 0)
            + dot(s_high, queries[m], 1, 0)
            + dot(a_low, dmixed, 1, 0)
            + dot(s_low, queries[m], 1, 0)
        )
        own_out[m] = total[:nodes]
        lower = total[nodes : nodes + reach].astype(bf16)
        upper = total[nodes + reach : nodes + 2 * reach].astype(bf16)
        even_out[m] = jnp.where(first, upper, lower)
        odd_out[m] = jnp.where(first, lower, upper)


def finish_kernel(side, own, even, odd, out):
    nodes, reach = own.shape[1], even.shape[1]
    first = side[0] == 0
    for m in range(own.shape[0]):
        e, o = even[m].astype(f32), odd[m].astype(f32)
        out[m, :reach] = (own[m, :reach] + jnp.where(first, o, e)).astype(bf16)
        out[m, reach : nodes - reach] = own[m, reach : nodes - reach].astype(bf16)
        out[m, nodes - reach :] = (own[m, nodes - reach :] + jnp.where(first, e, o)).astype(bf16)


def call(kernel, out_shape, args, scratch=(), name=None, scalars=0):
    vmem, smem = pl.BlockSpec(memory_space=pltpu.VMEM), pl.BlockSpec(memory_space=pltpu.SMEM)
    single = not isinstance(out_shape, (list, tuple))
    return pl.pallas_call(
        kernel,
        out_shape=out_shape,
        in_specs=[smem] * scalars + [vmem] * (len(args) - scalars),
        out_specs=vmem if single else [vmem] * len(out_shape),
        scratch_shapes=list(scratch),
        compiler_params=pltpu.CompilerParams(vmem_limit_bytes=VMEM_LIMIT),
        name=name,
    )(*args)


def add_up(terms, copies, name):
    return call(add_kernel, jax.ShapeDtypeStruct((copies,) + terms.shape[1:], bf16), (terms,), name=name)


def exchange(x, axes):
    return lax.all_to_all(x, axes, 0, 0, tiled=True)


def whole_exchange(x):
    return exchange(x, SPREAD)


def split_exchange(x):
    x = x.reshape((lax.axis_size(SPREAD[0]), -1) + x.shape[1:])
    x = exchange(x, SPREAD[:1])
    return lax.all_to_all(x, SPREAD[1:], 1, 1, tiled=True).reshape((-1,) + x.shape[2:])


def local(latents, queries, neighbours, truth, area_weight, var_weight, proj_weight):
    members, nodes, width = latents.shape
    points = queries.shape[1]
    variables = proj_weight.shape[1]
    reach = nodes // 4
    scale = 1.0 / math.sqrt(width)
    shards = lax.axis_size(SHARD)
    owners = lax.axis_size(MEMBER)
    share = points // owners
    forward = [(i, (i + 1) % shards) for i in range(shards)]
    backward = [(i, (i - 1) % shards) for i in range(shards)]

    low = lax.ppermute(latents[:, nodes - reach :], SHARD, forward)
    high = lax.ppermute(latents[:, :reach], SHARD, backward)

    first = lax.axis_index(SHARD) * nodes
    index = (neighbours.T - first + reach) % (nodes * shards)
    slots = jnp.where(
        index < reach, index + nodes, jnp.where(index < nodes + reach, index - reach, index)
    )
    weight = jnp.pad(proj_weight.T, ((0, LANES - variables), (0, 0)))
    start = lax.axis_index(MEMBER) * share
    pad_lanes = ((0, 0), (0, LANES - variables))
    target = jnp.pad(lax.dynamic_slice_in_dim(truth, start, share, 0), pad_lanes)
    area = lax.dynamic_slice_in_dim(area_weight, start, share, 0)
    weighting = jnp.pad(area[:, None] * var_weight[None, :], pad_lanes)

    window_rows = nodes + 2 * reach
    window = pltpu.VMEM((window_rows, width), bf16)
    core = lax.axis_index("core").astype(jnp.int32).reshape(1)
    swap = [(0, 1), (1, 0)]
    counts, near = call(
        prepare_kernel,
        [
            jax.ShapeDtypeStruct((window_rows, points), f32),
            jax.ShapeDtypeStruct((members, nodes, points), f32),
        ],
        (slots, latents, queries),
        name="prepare",
    )
    attn, keep, give, pred = call(
        functools.partial(forward_kernel, scale),
        [
            jax.ShapeDtypeStruct((members, window_rows, points), f32),
            jax.ShapeDtypeStruct((members, points, width // 2), bf16),
            jax.ShapeDtypeStruct((members, points, width // 2), bf16),
            jax.ShapeDtypeStruct((owners, members, share, LANES), f32),
        ],
        (core, counts, near, latents, low, high, queries, weight),
        [window],
        name="forward",
        scalars=1,
    )
    rows = exchange(pred, MEMBER)
    got = lax.ppermute(give, "core", swap)
    owner_grad = call(
        crps_kernel,
        jax.ShapeDtypeStruct((owners, 2 * members, share, LANES), bf16),
        (rows, target, weighting),
        name="crps",
    )
    grads = exchange(owner_grad, MEMBER)

    pieces = lax.axis_size(SPREAD)
    tall = width // 2 // pieces
    term = call(
        weight_kernel,
        jax.ShapeDtypeStruct((pieces, tall, LANES), bf16),
        (grads, keep, got),
        name="weight_term",
    )
    term = exchange(term, SPREAD)

    side = lax.axis_index("yhi").astype(jnp.int32).reshape(1)
    own_part, even_part, odd_part = call(
        functools.partial(backward_kernel, scale),
        [
            jax.ShapeDtypeStruct((members, nodes, width), f32),
            jax.ShapeDtypeStruct((members, reach, width), bf16),
            jax.ShapeDtypeStruct((members, reach, width), bf16),
        ],
        (side, grads, attn, latents, low, high, queries, weight),
        [window],
        name="backward",
        scalars=1,
    )
    term, even_part, odd_part = lax.optimization_barrier((term, even_part, odd_part))
    even_pairs = [(i, i ^ 1) for i in range(shards)]
    odd_pairs = [(i, (i + (1 if i % 2 else -1)) % shards) for i in range(shards)]
    odd_back = lax.ppermute(odd_part, SHARD, odd_pairs)
    even_back = lax.ppermute(even_part, SHARD, even_pairs)
    piece = exchange(add_up(term, lax.axis_size("z"), "add_plane"), "z")
    mine = lax.cond(var_weight[0] > 0.0, whole_exchange, split_exchange, add_up(piece, pieces, "add_z"))
    other = lax.ppermute(mine, "core", swap)
    proj_grad = call(
        assemble_kernel,
        jax.ShapeDtypeStruct((variables, width), f32),
        (core, mine, other),
        name="assemble",
        scalars=1,
    ).T

    latent_grad = call(
        finish_kernel,
        jax.ShapeDtypeStruct(latents.shape, bf16),
        (side, own_part, even_back, odd_back),
        name="finish",
        scalars=1,
    )
    return latent_grad, proj_grad


def solution(mesh):
    fine = Mesh(mesh.devices.reshape(4, 2, 12, 4, 2), MEMBER + SHARD)
    placed = (
        P(MEMBER, SHARD, None),
        P(MEMBER, SHARD, None),
        P(SHARD, None),
        P(SHARD, None),
        P(SHARD),
        P(),
        P(),
    )
    return jax.shard_map(
        local,
        mesh=fine,
        in_specs=placed,
        out_specs=(P(MEMBER, SHARD, None), P()),
        check_vma=False,
    )
```

```python
import functools
import math

import jax
import jax.numpy as jnp
from jax import lax
from jax.experimental import pallas as pl
from jax.experimental.pallas import tpu as pltpu
from jax.sharding import Mesh, PartitionSpec as P

smoothing = 0.25
fairness = 0.95
LANES = 128
f32, bf16 = jnp.float32, jnp.bfloat16

MEMBER = ("ylo", "core")
SHARD = ("z", "x", "yhi")
SPREAD = ("x", "ylo", "yhi")
VMEM_LIMIT = 48 * 1024 * 1024


def slope(diff):
    return diff * lax.rsqrt(diff * diff + smoothing * smoothing)


def dot(a, b, ca, cb):
    return lax.dot_general(a, b, (((ca,), (cb,)), ((), ())), preferred_element_type=f32)


def halves(x):
    high = x.astype(bf16)
    return high, (x - high.astype(f32)).astype(bf16)


def fill_window(window, m, own, low, high):
    nodes, reach = own.shape[1], low.shape[1]
    window[0:nodes] = own[m]
    window[nodes : nodes + reach] = low[m]
    window[nodes + reach : nodes + 2 * reach] = high[m]


def prepare_kernel(slots, own, queries, count_out, scores_out):
    rows, points = count_out.shape
    place = lax.broadcasted_iota(jnp.int32, (rows, points), 0)
    count = jnp.zeros((rows, points), f32)
    for slot in range(slots.shape[0]):
        count = count + (place == slots[slot : slot + 1]).astype(f32)
    count_out[...] = count
    for m in range(queries.shape[0]):
        scores_out[m] = dot(own[m], queries[m], 1, 1)


def forward_kernel(
    scale, core, counts, near, own, low, high, queries, weight,
    attn_out, keep_out, give_out, pred_out, window,
):
    members, points, width = queries.shape
    half = width // 2
    here = core[0] == 0
    nodes = own.shape[1]
    share = pred_out.shape[2]
    count = counts[...]
    used = count > 0.0
    for m in range(members):
        fill_window(window, m, own, low, high)
        scores = jnp.concatenate([near[m], dot(window[nodes:], queries[m], 1, 1)]) * scale
        scores = jnp.where(used, scores, -1e30)
        top = jnp.max(scores, axis=0, keepdims=True)
        raised = count * jnp.exp(scores - top)
        attn = raised / jnp.sum(raised, axis=0, keepdims=True)
        attn_out[m] = attn
        attn_high, attn_low = halves(attn)
        mixed = queries[m].astype(f32) + (
            dot(attn_high, window[...], 0, 0) + dot(attn_low, window[...], 0, 0)
        )
        mixed = mixed.astype(bf16)
        left, right = mixed[:, :half], mixed[:, half:]
        keep_out[m] = jnp.where(here, left, right)
        give_out[m] = jnp.where(here, right, left)
        pred = dot(mixed, weight[...], 1, 1)
        for k in range(points // share):
            pred_out[k, m] = pred[k * share : (k + 1) * share]


def crps_kernel(rows, target, weighting, out):
    groups, each, share, lanes = rows.shape
    count = groups * each
    eps_fair = (1.0 - fairness) / count
    values = [rows[k // each, k % each] for k in range(count)]
    spread = [jnp.zeros((share, lanes), f32) for _ in range(count)]
    for a in range(count):
        for b in range(a + 1, count):
            s = slope(values[a] - values[b])
            spread[a] = spread[a] + s
            spread[b] = spread[b] - s
    for k in range(count):
        skill = slope(values[k] - target[...])
        grad = weighting[...] * (
            skill / count - (1.0 - eps_fair) / (count * (count - 1)) * spread[k]
        )
        grad = grad.astype(bf16)
        group, m = k // each, k % each
        out[group, m] = grad
        out[group ^ 1, each + m] = grad


def weight_kernel(grads, keep, got, out):
    owners, _, share, lanes = grads.shape
    members = keep.shape[0]
    points = owners * share
    total = None
    for m in range(members):
        for part, mixed in ((m, keep), (members + m, got)):
            g = grads[:, part].reshape(points, lanes)
            term = dot(g, mixed[m], 0, 0)
            total = term if total is None else total + term
    pieces, high, wide = out.shape
    across = total.shape[1] // wide
    for k in range(pieces):
        r, c = k // across * high, k % across * wide
        out[k] = total[r : r + high, c : c + wide].astype(bf16)


def add_kernel(terms, out):
    total = terms[0].astype(f32)
    for k in range(1, terms.shape[0]):
        total = total + terms[k].astype(f32)
    total = total.astype(bf16)
    for k in range(out.shape[0]):
        out[k] = total


def assemble_kernel(core, mine, other, out):
    pieces, high, wide = mine.shape
    half = out.shape[1] // 2
    across = half // wide
    here = core[0] == 0
    for k in range(pieces):
        r, c = k // across * high, k % across * wide
        size = min(high, out.shape[0] - r)
        if size > 0:
            a, b = mine[k].astype(f32)[:size], other[k].astype(f32)[:size]
            out[r : r + size, c : c + wide] = jnp.where(here, a, b)
            out[r : r + size, half + c : half + c + wide] = jnp.where(here, b, a)


def backward_kernel(
    scale, side, grads, attn, own, low, high, queries, weight, own_out, even_out, odd_out, window
):
    first = side[0] == 0
    owners, _, share, lanes = grads.shape
    members = queries.shape[0]
    points = owners * share
    nodes, reach = own.shape[1], low.shape[1]
    for m in range(members):
        fill_window(window, m, own, low, high)
        g = grads[:, m].reshape(points, lanes)
        dmixed = dot(g, weight[...], 1, 0).astype(bf16)
        dattn = dot(window[...], dmixed, 1, 1)
        a = attn[m]
        dscores = a * (dattn - jnp.sum(a * dattn, axis=0, keepdims=True)) * scale
        a_high, a_low = halves(a)
        s_high, s_low = halves(dscores)
        total = (
            dot(a_high, dmixed, 1, 0)
            + dot(s_high, queries[m], 1, 0)
            + dot(a_low, dmixed, 1, 0)
            + dot(s_low, queries[m], 1, 0)
        )
        own_out[m] = total[:nodes]
        lower = total[nodes : nodes + reach].astype(bf16)
        upper = total[nodes + reach : nodes + 2 * reach].astype(bf16)
        even_out[m] = jnp.where(first, upper, lower)
        odd_out[m] = jnp.where(first, lower, upper)


def finish_kernel(side, own, even, odd, out):
    nodes, reach = own.shape[1], even.shape[1]
    first = side[0] == 0
    for m in range(own.shape[0]):
        e, o = even[m].astype(f32), odd[m].astype(f32)
        out[m, :reach] = (own[m, :reach] + jnp.where(first, o, e)).astype(bf16)
        out[m, reach : nodes - reach] = own[m, reach : nodes - reach].astype(bf16)
        out[m, nodes - reach :] = (own[m, nodes - reach :] + jnp.where(first, e, o)).astype(bf16)


def call(kernel, out_shape, args, scratch=(), name=None, scalars=0):
    vmem, smem = pl.BlockSpec(memory_space=pltpu.VMEM), pl.BlockSpec(memory_space=pltpu.SMEM)
    single = not isinstance(out_shape, (list, tuple))
    return pl.pallas_call(
        kernel,
        out_shape=out_shape,
        in_specs=[smem] * scalars + [vmem] * (len(args) - scalars),
        out_specs=vmem if single else [vmem] * len(out_shape),
        scratch_shapes=list(scratch),
        compiler_params=pltpu.CompilerParams(vmem_limit_bytes=VMEM_LIMIT),
        name=name,
    )(*args)


def add_up(terms, copies, name):
    return call(add_kernel, jax.ShapeDtypeStruct((copies,) + terms.shape[1:], bf16), (terms,), name=name)


def exchange(x, axes):
    return lax.all_to_all(x, axes, 0, 0, tiled=True)


def whole_exchange(x):
    return exchange(x, SPREAD)


def split_exchange(x):
    x = x.reshape((lax.axis_size(SPREAD[0]), -1) + x.shape[1:])
    x = exchange(x, SPREAD[:1])
    return lax.all_to_all(x, SPREAD[1:], 1, 1, tiled=True).reshape((-1,) + x.shape[2:])


def local(latents, queries, neighbours, truth, area_weight, var_weight, proj_weight):
    members, nodes, width = latents.shape
    points = queries.shape[1]
    variables = proj_weight.shape[1]
    reach = nodes // 4
    scale = 1.0 / math.sqrt(width)
    shards = lax.axis_size(SHARD)
    owners = lax.axis_size(MEMBER)
    share = points // owners
    forward = [(i, (i + 1) % shards) for i in range(shards)]
    backward = [(i, (i - 1) % shards) for i in range(shards)]

    low = lax.ppermute(latents[:, nodes - reach :], SHARD, forward)
    high = lax.ppermute(lax.optimization_barrier(latents)[:, :reach], SHARD, backward)

    first = lax.axis_index(SHARD) * nodes
    index = (neighbours.T - first + reach) % (nodes * shards)
    slots = jnp.where(
        index < reach, index + nodes, jnp.where(index < nodes + reach, index - reach, index)
    )
    weight = jnp.pad(proj_weight.T, ((0, LANES - variables), (0, 0)))
    start = lax.axis_index(MEMBER) * share
    pad_lanes = ((0, 0), (0, LANES - variables))
    target = jnp.pad(lax.dynamic_slice_in_dim(truth, start, share, 0), pad_lanes)
    area = lax.dynamic_slice_in_dim(area_weight, start, share, 0)
    weighting = jnp.pad(area[:, None] * var_weight[None, :], pad_lanes)

    window_rows = nodes + 2 * reach
    window = pltpu.VMEM((window_rows, width), bf16)
    core = lax.axis_index("core").astype(jnp.int32).reshape(1)
    swap = [(0, 1), (1, 0)]
    counts, near = call(
        prepare_kernel,
        [
            jax.ShapeDtypeStruct((window_rows, points), f32),
            jax.ShapeDtypeStruct((members, nodes, points), f32),
        ],
        (slots, latents, queries),
        name="prepare",
    )
    attn, keep, give, pred = call(
        functools.partial(forward_kernel, scale),
        [
            jax.ShapeDtypeStruct((members, window_rows, points), f32),
            jax.ShapeDtypeStruct((members, points, width // 2), bf16),
            jax.ShapeDtypeStruct((members, points, width // 2), bf16),
            jax.ShapeDtypeStruct((owners, members, share, LANES), f32),
        ],
        (core, counts, near, latents, low, high, queries, weight),
        [window],
        name="forward",
        scalars=1,
    )
    rows = exchange(pred, MEMBER)
    got = lax.ppermute(give, "core", swap)
    owner_grad = call(
        crps_kernel,
        jax.ShapeDtypeStruct((owners, 2 * members, share, LANES), bf16),
        (rows, target, weighting),
        name="crps",
    )
    grads = exchange(owner_grad, MEMBER)

    pieces = lax.axis_size(SPREAD)
    tall = width // 2 // pieces
    term = call(
        weight_kernel,
        jax.ShapeDtypeStruct((pieces, tall, LANES), bf16),
        (grads, keep, got),
        name="weight_term",
    )
    term = exchange(term, SPREAD)

    side = lax.axis_index("yhi").astype(jnp.int32).reshape(1)
    own_part, even_part, odd_part = call(
        functools.partial(backward_kernel, scale),
        [
            jax.ShapeDtypeStruct((members, nodes, width), f32),
            jax.ShapeDtypeStruct((members, reach, width), bf16),
            jax.ShapeDtypeStruct((members, reach, width), bf16),
        ],
        (side, grads, attn, latents, low, high, queries, weight),
        [window],
        name="backward",
        scalars=1,
    )
    term, even_part, odd_part = lax.optimization_barrier((term, even_part, odd_part))
    even_pairs = [(i, i ^ 1) for i in range(shards)]
    odd_pairs = [(i, (i + (1 if i % 2 else -1)) % shards) for i in range(shards)]
    odd_back = lax.ppermute(odd_part, SHARD, odd_pairs)
    even_back = lax.ppermute(even_part, SHARD, even_pairs)
    piece = exchange(add_up(term, lax.axis_size("z"), "add_plane"), "z")
    mine = lax.cond(var_weight[0] > 0.0, whole_exchange, split_exchange, add_up(piece, pieces, "add_z"))
    other = lax.ppermute(mine, "core", swap)
    proj_grad = call(
        assemble_kernel,
        jax.ShapeDtypeStruct((variables, width), f32),
        (core, mine, other),
        name="assemble",
        scalars=1,
    ).T

    latent_grad = call(
        finish_kernel,
        jax.ShapeDtypeStruct(latents.shape, bf16),
        (side, own_part, even_back, odd_back),
        name="finish",
        scalars=1,
    )
    return latent_grad, proj_grad


def solution(mesh):
    fine = Mesh(mesh.devices.reshape(4, 2, 12, 4, 2), MEMBER + SHARD)
    placed = (
        P(MEMBER, SHARD, None),
        P(MEMBER, SHARD, None),
        P(SHARD, None),
        P(SHARD, None),
        P(SHARD),
        P(),
        P(),
    )
    return jax.shard_map(
        local,
        mesh=fine,
        in_specs=placed,
        out_specs=(P(MEMBER, SHARD, None), P()),
        check_vma=False,
    )
```
